256 devices in a mesh: prow: 32 (over z, x), pcol: 8 (over y, core).
Axes of the slice: x: 4, y: 4, z: 8, core: 2. Of those that a mesh axis runs over, the one named last changes fastest.
Arguments:
- matrix: bfloat16 [1, 16384, 4, 4096], P(None, 'prow', None, 'pcol'), may hold values from -6 to 6
- upper_inverse: bfloat16 [4, 512, 512], replicated, may hold values from -1.8 to 1.8
- lower_inverse: bfloat16 [4, 512, 512], replicated, may hold values from -0.079549513 to 0.079549513
- structure: int32 [32, 32], replicated, may hold values 0 or 1
Outputs:
- factored: float32 [1, 16384, 4, 4096], P(None, 'prow', None, 'pcol')
The draws below stay inside these ranges and needn't reach their ends.
All inputs are finite; a program needn't handle non-finite values.
Results may differ from the reference program's by a relative error of at most 0.012.
Values may be sent and summed in bfloat16 or wider, within the bound.
No kernel may reach another device: no remote copies, remote signals or barrier semaphores. Data moves between devices by JAX's collectives and lax.ppermute only.
A program may use at most 64 MiB of HBM per device.

```python
import jax
import jax.numpy as jnp
from jax import lax

B = 512
RB = 1
STEPS = 4
NB = 32
CB = 4
N_PROW = 32
N_PCOL = 8


def dominant_operator(key, low, high, spread):
    diag_key, rest_key = jax.random.split(key)
    diagonal = jnp.exp(jax.random.uniform(diag_key, (STEPS, B), jnp.float32, jnp.log(low), jnp.log(high)))
    rest = jnp.clip(jax.random.normal(rest_key, (STEPS, B, B), jnp.float32), -4.0, 4.0)
    rest = rest * (spread / B ** 0.5)
    identity = (jnp.arange(B)[:, None] == jnp.arange(B)[None, :]).astype(jnp.float32)
    return diagonal[:, :, None] * identity[None] + rest * (1.0 - identity[None])


def draw_upper_inverse(key, part):
    key = jax.random.fold_in(key, 11)
    operator = dominant_operator(key, 0.8, 1.6, 0.35)
    return operator.astype(jnp.bfloat16)


def draw_lower_inverse(key, part):
    key = jax.random.fold_in(key, 23)
    operator = dominant_operator(key, 0.8, 1.6, 0.35)
    return (operator / B ** 0.5).astype(jnp.bfloat16)


def set_ends(array, stream_key, low, largest):
    extent = array.shape
    place = [jax.random.randint(jax.random.fold_in(stream_key, axis), (), 0, extent[axis]) for axis in range(len(extent))]
    array = array.at[tuple(place)].set(low)
    longest = extent.index(max(extent))
    place[longest] = (place[longest] + 1) % extent[longest]
    return array.at[tuple(place)].set(largest)


def shard_levels(rng, dims, pieces, low, top_value):
    def one(axis_at, parts):
        steps = jax.random.uniform(jax.random.fold_in(jax.random.fold_in(rng, 6), axis_at), (parts,), jnp.float32, low / len(pieces), top_value / len(pieces))
        return jnp.repeat(jnp.exp(steps), dims[axis_at] // parts).reshape((-1,) + (1,) * (len(dims) - axis_at - 1))

    factor_of = one(*pieces[0])
    for cut in pieces[1:]:
        factor_of = factor_of * one(*cut)
    return factor_of


def bell_draw(own_key, extent, scale, reach, cuts=(), dtype=jnp.bfloat16):
    factor_of = shard_levels(own_key, extent, cuts, -0.22, 0.18) if cuts else 1.0
    values = jax.random.normal(own_key, extent, jnp.float32) * scale * factor_of
    return jnp.minimum(jnp.maximum(values, -reach), reach).astype(dtype)


def setup_inputs(seed: int = 0) -> dict:
    key_of = jax.random.split(jax.random.key(seed), 5)
    return {
        "matrix": bell_draw(key_of[0], (RB, N_PROW * B, CB, N_PCOL * B), 1.0, 6.0, ((1, 32), (3, 8))),
        "upper_inverse": draw_upper_inverse(jax.random.fold_in(key_of[4], 71), 0),
        "lower_inverse": draw_lower_inverse(jax.random.fold_in(key_of[4], 71), 0),
        "structure": set_ends((jax.random.randint(key_of[3], (NB, NB), 0, 5) < 3).astype(jnp.int32), jax.random.fold_in(key_of[3], 1), 0, 1),
    }


def reference(matrix, upper_inverse, lower_inverse, structure):
    nblocks = RB * N_PROW
    state = matrix.astype(jnp.float32).reshape(nblocks, B, nblocks, B)
    block_ids = jnp.arange(nblocks)
    shape_f = structure.astype(jnp.float32)
    for k in range(STEPS):
        later = (block_ids > k).astype(jnp.float32)
        below = shape_f[:, k] * later
        right = shape_f[k, :] * later
        column = state[:, :, k, :].astype(jnp.bfloat16).astype(jnp.float32)
        lower = (jnp.einsum('iab,bc->iac', column, upper_inverse[k].astype(jnp.float32)) * below[:, None, None]).astype(jnp.bfloat16)
        row_now = state[k].astype(jnp.bfloat16).astype(jnp.float32)
        upper = (jnp.einsum('ab,bjc->ajc', lower_inverse[k].astype(jnp.float32), row_now) * right[None, :, None]).astype(jnp.bfloat16)
        keep = shape_f * later[:, None] * later[None, :]
        upper_f = upper.astype(jnp.float32)

        def one_row(items):
            left_block, keep_row = items
            return jnp.einsum('ab,bjc->ajc', left_block.astype(jnp.float32), upper_f) * keep_row[None, :, None]

        product = lax.map(one_row, (lower, keep))
        state = state - product
        lower_f = lower.astype(jnp.float32)
        state = state.at[:, :, k, :].set(jnp.where((block_ids > k)[:, None, None], lower_f, state[:, :, k, :]))
        state = state.at[k].set(jnp.where((block_ids > k)[None, :, None], upper_f, state[k]))
    return state.reshape(RB, N_PROW * B, CB, N_PCOL * B)
```

```python
import functools

import jax
import jax.numpy as jnp
from jax import lax
from jax.experimental import pallas as pl
from jax.experimental.pallas import tpu as pltpu
from jax.sharding import PartitionSpec as P

STEPS = 4
HALF = jnp.bfloat16
FULL = jnp.float32
VMEM_LIMIT = 56 * 1024 * 1024


def mm(a, b):
    return jnp.dot(a, b, preferred_element_type=FULL)


def factor_kernel(ids, shape, mine, other, row, v, w, low, left, up):
    n = v.shape[1]
    p = ids[0]
    core = ids[2]

    def raw(i, j):
        a = jnp.concatenate([mine[z * 4 + i, 4 + j % 2] for z in range(8)], axis=0)
        b = jnp.concatenate([other[z * 4 + i, j % 2] for z in range(8)], axis=0)
        return jnp.where(core == j // 2, a, b)

    def cut(k):
        return slice(k * n, (k + 1) * n)

    for k in range(3):
        for i in range(k + 1, 4):
            block = raw(i, k)
            if k:
                block = (block.astype(FULL) - mm(low[i - 1, :, 0 : k * n], up[0 : k * n, cut(k)])).astype(HALF)
            low[i - 1, :, cut(k)] = (mm(block, v[k]) * shape[i, k].astype(FULL)).astype(HALF)
        for j in range(k + 1, 4):
            block = raw(k, j)
            if k:
                block = (block.astype(FULL) - mm(low[k - 1, :, 0 : k * n], up[0 : k * n, cut(j)])).astype(HALF)
            up[cut(k), cut(j)] = (mm(w[k], block) * shape[k, j].astype(FULL)).astype(HALF)
    for k in range(4):
        block = row[k]
        if k:
            block = (block.astype(FULL) - mm(left[:, 0 : k * n], up[0 : k * n, cut(k)])).astype(HALF)
        scale = jnp.where(p > k, shape[p, k], 0).astype(FULL)
        left[:, cut(k)] = (mm(block, v[k]) * scale).astype(HALF)


def column_kernel(ids, shape, raw, own, low, left, w, out, upper):
    n = w.shape[1]
    p, q = ids[0], ids[1]
    c = pl.program_id(0)
    j = c * 8 + q
    for k in range(4):
        block = jnp.concatenate([raw[z * 4 + k, 0] for z in range(8)], axis=0)
        if k:
            block = (block.astype(FULL) - mm(low[k - 1, :, 0 : k * n], upper[0 : k * n, :])).astype(HALF)
        scale = jnp.where(j > k, shape[k, j], 0).astype(FULL)
        upper[k * n : (k + 1) * n, :] = (mm(w[k], block) * scale).astype(HALF)
    keep = shape[p, j].astype(FULL)
    out[0] = own[0].astype(FULL) - keep * mm(left[...], upper[...])

    @pl.when(jnp.logical_and(p < STEPS, j > p))
    def _():
        out[0] = upper[pl.ds(pl.multiple_of(jnp.minimum(p, 3) * n, n), n), :].astype(FULL)

    @pl.when(jnp.logical_and(j < STEPS, p > j))
    def _():
        out[0] = left[:, pl.ds(pl.multiple_of(jnp.minimum(j, 3) * n, n), n)].astype(FULL)


def factor(ids, shape, mine, other, row, v, w):
    n = v.shape[1]
    vmem = pl.BlockSpec(memory_space=pltpu.VMEM)
    smem = pl.BlockSpec(memory_space=pltpu.SMEM)
    return pl.pallas_call(
        factor_kernel,
        out_shape=(
            jax.ShapeDtypeStruct((3, n, 3 * n), HALF),
            jax.ShapeDtypeStruct((n, 4 * n), HALF),
        ),
        in_specs=[smem, smem, vmem, vmem, vmem, vmem, vmem],
        out_specs=(vmem, vmem),
        scratch_shapes=[pltpu.VMEM((3 * n, 4 * n), HALF)],
        compiler_params=pltpu.CompilerParams(vmem_limit_bytes=VMEM_LIMIT),
        cost_estimate=pl.CostEstimate(flops=60 * n**3, bytes_accessed=18 * 2**20, transcendentals=0),
    )(ids, shape, mine, other, row, v, w)


def columns(ids, shape, raw, own, low, left, w):
    n = w.shape[1]
    smem = pl.BlockSpec(memory_space=pltpu.SMEM)
    whole = lambda a: pl.BlockSpec(a.shape, lambda c: (0,) * a.ndim)
    return pl.pallas_call(
        column_kernel,
        grid=(4,),
        out_shape=jax.ShapeDtypeStruct((4, n, n), FULL),
        in_specs=[
            smem,
            smem,
            pl.BlockSpec((32, 1, n // 8, n), lambda c: (0, c, 0, 0)),
            pl.BlockSpec((1, n, n), lambda c: (c, 0, 0)),
            whole(low),
            whole(left),
            whole(w),
        ],
        out_specs=pl.BlockSpec((1, n, n), lambda c: (c, 0, 0)),
        scratch_shapes=[pltpu.VMEM((4 * n, n), HALF)],
        compiler_params=pltpu.CompilerParams(vmem_limit_bytes=VMEM_LIMIT),
        cost_estimate=pl.CostEstimate(flops=112 * n**3, bytes_accessed=24 * 2**20, transcendentals=0),
    )(ids, shape, raw, own, low, left, w)


def on_device(matrix, upper_inverse, lower_inverse, structure):
    p = lax.axis_index("prow")
    q = lax.axis_index("pcol")
    z = p // 4
    core = lax.rem(q, 2)
    n = matrix.shape[1]
    part = n // 8
    own = jnp.transpose(matrix[0], (1, 0, 2))
    ids = jnp.stack([p, q, core]).astype(jnp.int32)

    piece = own[:, :part]
    for s in range(1, 8):
        to = [(x, x + 4 * s) for x in range(4)]
        came = lax.ppermute(own[:, s * part : (s + 1) * part], "prow", to)
        piece = jnp.where(z == s, came, piece)

    row = lax.all_gather(own[0], "pcol")[:4]

    corner = lax.all_gather(piece[0], "pcol")
    corner = jnp.where(core == 0, corner[0:2], corner[2:4])

    raw = lax.all_gather(jnp.concatenate([piece, corner], axis=0), "prow")
    other = lax.ppermute(raw[:, 4:6], "pcol", [(i, i ^ 1) for i in range(8)])

    low, left = factor(ids, structure, raw, other, row, upper_inverse, lower_inverse)
    out = columns(ids, structure, raw, own, low, left, lower_inverse)
    return jnp.transpose(out, (1, 0, 2))[None]


def solution(mesh):
    return jax.shard_map(
        on_device,
        mesh=mesh,
        in_specs=(P(None, "prow", None, "pcol"), P(), P(), P()),
        out_specs=P(None, "prow", None, "pcol"),
        check_vma=False,
    )
```

```python
import functools

import jax
import jax.numpy as jnp
from jax import lax
from jax.experimental import pallas as pl
from jax.experimental.pallas import tpu as pltpu
from jax.sharding import PartitionSpec as P

STEPS = 4
HALF = jnp.bfloat16
FULL = jnp.float32
VMEM_LIMIT = 56 * 1024 * 1024


def mm(a, b):
    return jnp.dot(a, b, preferred_element_type=FULL)


def shift(block, way):
    move = 1 if way[-1] == "+" else -1
    if way[0] == "z":
        return lax.ppermute(block, "prow", [(i, (i + 4 * move) % 32) for i in range(32)])
    if way[0] == "x":
        return lax.ppermute(block, "prow", [(i, i // 4 * 4 + (i + move) % 4) for i in range(32)])
    if way[0] == "y":
        return lax.ppermute(block, "pcol", [(i, (i + 2 * move) % 8) for i in range(8)])
    return lax.ppermute(block, "pcol", [(i, i ^ 1) for i in range(8)])


def around_four(block, axis):
    half = block.shape[0] // 2
    above = shift(block, axis + "-")
    below = shift(block, axis + "+")
    far = [shift(below[:half], axis + "+"), shift(above[half:], axis + "-")]
    return [block, above, jnp.concatenate(far, axis=0), below]


def around_eight(block):
    half = block.shape[1] // 2
    up, down = [block], [block]
    for _ in range(3):
        up.append(shift(up[-1], "z+"))
        down.append(shift(down[-1], "z-"))
    far = [shift(up[3][:, :half], "z+"), shift(down[3][:, half:], "z-")]
    return up + [jnp.concatenate(far, axis=1)] + down[:0:-1]


def kernel(ids, shape, mine, other, row_mine, row_other, v, w, raw, own, out, low, left, up, upper):
    n = v.shape[1]
    p, q = ids[0], ids[1]
    z, x, y, core = p // 4, lax.rem(p, 4), q // 2, lax.rem(q, 2)
    c = pl.program_id(0)
    j = c * 8 + q

    def cut(k):
        return slice(k * n, (k + 1) * n)

    def raw_corner(k, m):
        dx, dy, gap = lax.rem(k - x + 4, 4), lax.rem(m - y + 4, 4), lax.rem(m - x + 4, 4)
        at = jnp.where(dx < gap, dx, jnp.maximum(dx - 1, 0))
        parts = []
        for i in range(8):
            away = lax.rem(z - i + 8, 8)
            here, there = mine[dy, away, at], other[dy, away, at]
            parts += [jnp.where(core == 0, here, there), jnp.where(core == 0, there, here)]
        return jnp.concatenate(parts, axis=0)

    def raw_row(k):
        dy = lax.rem(k // 2 - y + 4, 4)
        return jnp.where(core == k % 2, row_mine[dy], row_other[dy])

    @pl.when(c == 0)
    def _():
        for k in range(3):
            for i in range(k + 1, 4):
                block = raw_corner(i, k)
                if k:
                    block = (block.astype(FULL) - mm(low[i - 1, :, 0 : k * n], up[0 : k * n, cut(k)])).astype(HALF)
                low[i - 1, :, cut(k)] = (mm(block, v[k]) * shape[i, k].astype(FULL)).astype(HALF)
            for i in range(k + 1, 4):
                block = raw_corner(k, i)
                if k:
                    block = (block.astype(FULL) - mm(low[k - 1, :, 0 : k * n], up[0 : k * n, cut(i)])).astype(HALF)
                up[cut(k), cut(i)] = (mm(w[k], block) * shape[k, i].astype(FULL)).astype(HALF)
        for k in range(4):
            block = raw_row(k)
            if k:
                block = (block.astype(FULL) - mm(left[:, 0 : k * n], up[0 : k * n, cut(k)])).astype(HALF)
            scale = jnp.where(p > k, shape[p, k], 0).astype(FULL)
            left[:, cut(k)] = (mm(block, v[k]) * scale).astype(HALF)

    for k in range(4):
        block = jnp.concatenate([raw[i * 4 + k, 0] for i in range(8)], axis=0)
        if k:
            block = (block.astype(FULL) - mm(low[k - 1, :, 0 : k * n], upper[0 : k * n, :])).astype(HALF)
        scale = jnp.where(j > k, shape[k, j], 0).astype(FULL)
        upper[cut(k), :] = (mm(w[k], block) * scale).astype(HALF)
    keep = shape[p, j].astype(FULL)
    out[0] = own[0].astype(FULL) - keep * mm(left[...], upper[...])

    @pl.when(jnp.logical_and(p < STEPS, j > p))
    def _():
        out[0] = upper[pl.ds(pl.multiple_of(jnp.minimum(p, 3) * n, n), n), :].astype(FULL)

    @pl.when(jnp.logical_and(j < STEPS, p > j))
    def _():
        out[0] = left[:, pl.ds(pl.multiple_of(jnp.minimum(j, 3) * n, n), n)].astype(FULL)


def factor_and_update(ids, shape, corner, row, v, w, raw, own):
    n = w.shape[1]
    smem = pl.BlockSpec(memory_space=pltpu.SMEM)
    whole = lambda a: pl.BlockSpec(a.shape, lambda c: (0,) * a.ndim, pipeline_mode=pl.Buffered(1))
    return pl.pallas_call(
        kernel,
        grid=(4,),
        out_shape=jax.ShapeDtypeStruct((4, n, n), FULL),
        in_specs=[smem, smem]
        + [whole(a) for a in (*corner, *row, v, w)]
        + [
            pl.BlockSpec((32, 1, n // 8, n), lambda c: (0, c, 0, 0)),
            pl.BlockSpec((1, n, n), lambda c: (c, 0, 0)),
        ],
        out_specs=pl.BlockSpec((1, n, n), lambda c: (c, 0, 0)),
        scratch_shapes=[
            pltpu.VMEM((3, n, 3 * n), HALF),
            pltpu.VMEM((n, 4 * n), HALF),
            pltpu.VMEM((3 * n, 4 * n), HALF),
            pltpu.VMEM((4 * n, n), HALF),
        ],
        compiler_params=pltpu.CompilerParams(vmem_limit_bytes=VMEM_LIMIT),
        cost_estimate=pl.CostEstimate(flops=172 * n**3, bytes_accessed=30 * 2**20, transcendentals=0),
    )(ids, shape, *corner, *row, v, w, raw, own)


def on_device(matrix, upper_inverse, lower_inverse, structure):
    p = lax.axis_index("prow")
    q = lax.axis_index("pcol")
    z, core = p // 4, lax.rem(q, 2)
    n = matrix.shape[1]
    part = n // 8
    own = jnp.transpose(matrix[0], (1, 0, 2))
    ids = jnp.stack([p, q]).astype(jnp.int32)

    piece = own[:, :part]
    came = {}
    for s in (1, 4, 5, 3, 6, 2, 7):
        to = [(i, i + 4 * s) for i in range(4)]
        came[s] = lax.ppermute(own[:, s * part : (s + 1) * part], "prow", to)
    row, came[1] = lax.optimization_barrier((own[0], came[1]))
    above, below = shift(row, "y-"), shift(row, "y+")
    for s in came:
        piece = jnp.where(z == s, came[s], piece)

    raw = lax.all_gather(piece, "prow")

    seed, above, below = lax.optimization_barrier((piece[0], above, below))
    first = lax.ppermute(seed[: part // 2], "pcol", [(i, 2 * i) for i in range(4)])
    second = lax.ppermute(seed[part // 2 :], "pcol", [(i, 2 * i + 1) for i in range(4)])
    corner = jnp.where(core == 0, first, second)
    corner = [corner, shift(corner, "x-"), shift(shift(corner, "x-"), "x-"), shift(corner, "x+")]
    gap = lax.rem(q // 2 - p % 4 + 4, 4)
    corner = jnp.stack([jnp.where(i < gap, corner[i], corner[i + 1]) for i in range(3)])
    far = [shift(below[: n // 2], "y+"), shift(above[n // 2 :], "y-")]
    row = jnp.stack([row, above, jnp.concatenate(far, axis=0), below])
    corner = jnp.stack(around_eight(corner))
    corner, row = lax.optimization_barrier((corner, row))
    row = [row, shift(row, "c")]
    corner = jnp.stack(around_four(corner, "y"))
    corner = [corner, shift(corner, "c")]

    out = factor_and_update(ids, structure, corner, row, upper_inverse, lower_inverse, raw, own)
    return jnp.transpose(out, (1, 0, 2))[None]


def solution(mesh):
    return jax.shard_map(
        on_device,
        mesh=mesh,
        in_specs=(P(None, "prow", None, "pcol"), P(), P(), P()),
        out_specs=P(None, "prow", None, "pcol"),
        check_vma=False,
    )
```

```python
import functools

import jax
import jax.numpy as jnp
from jax import lax
from jax.experimental import pallas as pl
from jax.experimental.pallas import tpu as pltpu
from jax.sharding import PartitionSpec as P

STEPS = 4
HALF = jnp.bfloat16
FULL = jnp.float32
VMEM_LIMIT = 56 * 1024 * 1024


def mm(a, b):
    return jnp.dot(a, b, preferred_element_type=FULL)


def shift(block, way):
    move = 1 if way[-1] == "+" else -1
    if way[0] == "z":
        return lax.ppermute(block, "prow", [(i, (i + 4 * move) % 32) for i in range(32)])
    if way[0] == "x":
        return lax.ppermute(block, "prow", [(i, i // 4 * 4 + (i + move) % 4) for i in range(32)])
    if way[0] == "y":
        return lax.ppermute(block, "pcol", [(i, (i + 2 * move) % 8) for i in range(8)])
    return lax.ppermute(block, "pcol", [(i, i ^ 1) for i in range(8)])


def around_eight(block):
    half = block.shape[1] // 2
    up, down = [block], [block]
    for _ in range(3):
        up.append(shift(up[-1], "z+"))
        down.append(shift(down[-1], "z-"))
    far = [shift(up[3][:, :half], "z+"), shift(down[3][:, half:], "z-")]
    return up + [jnp.concatenate(far, axis=1)] + down[:0:-1]


def cut(k, n):
    return slice(k * n, (k + 1) * n)


def factor_kernel(ids, shape, *refs):
    mine, other, (row_mine, row_other, v, w, low, left, up) = refs[:4], refs[4:8], refs[8:]
    n = v.shape[1]
    p, q = ids[0], ids[1]
    z, x, y, core = p // 4, lax.rem(p, 4), q // 2, lax.rem(q, 2)

    def raw_corner(k, m):
        dx, dy, gap = lax.rem(k - x + 4, 4), lax.rem(m - y + 4, 4), lax.rem(m - x + 4, 4)
        at = jnp.where(dx < gap, dx, jnp.maximum(dx - 1, 0))
        odd, upper_half = lax.rem(dy, 2) == 1, dy >= 2

        def pick(four, away):
            low_pair = jnp.where(odd, four[1][away, at], four[0][away, at])
            return jnp.where(upper_half, jnp.where(odd, four[3][away, at], four[2][away, at]), low_pair)

        parts = []
        for i in range(8):
            away = lax.rem(z - i + 8, 8)
            here, there = pick(mine, away), pick(other, away)
            parts += [jnp.where(core == 0, here, there), jnp.where(core == 0, there, here)]
        return jnp.concatenate(parts, axis=0)

    def raw_row(k):
        dy = lax.rem(k // 2 - y + 4, 4)
        return jnp.where(core == k % 2, row_mine[dy], row_other[dy])

    def fill(ref, rows, cols, present, make):
        @pl.when(present)
        def _():
            ref[rows, cols] = make().astype(HALF)

        @pl.when(jnp.logical_not(present))
        def _():
            ref[rows, cols] = jnp.zeros((n, n), HALF)

    def less(block, a, b):
        return (block.astype(FULL) - mm(a, b)).astype(HALF)

    for k in range(3):
        for i in range(k + 1, 4):

            def make_low():
                block = raw_corner(i, k)
                if k:
                    block = less(block, low[i - 1, :, 0 : k * n], up[0 : k * n, cut(k, n)])
                return mm(block, v[k])

            def make_up():
                block = raw_corner(k, i)
                if k:
                    block = less(block, low[k - 1, :, 0 : k * n], up[0 : k * n, cut(i, n)])
                return mm(w[k], block)

            fill(low.at[i - 1], slice(None), cut(k, n), shape[i, k] != 0, make_low)
            fill(up, cut(k, n), cut(i, n), shape[k, i] != 0, make_up)
    for k in range(4):

        def make_left():
            block = raw_row(k)
            if k:
                block = less(block, left[:, 0 : k * n], up[0 : k * n, cut(k, n)])
            return mm(block, v[k])

        fill(left, slice(None), cut(k, n), jnp.logical_and(p > k, shape[p, k] != 0), make_left)


def column_kernel(ids, shape, raw, own, low, left, w, whole_out, upper, out):
    n = w.shape[1]
    p, q = ids[0], ids[1]
    c = pl.program_id(0)
    j = c * 8 + q
    for k in range(4):
        present = jnp.logical_and(j > k, shape[k, j] != 0)

        @pl.when(present)
        def _():
            block = jnp.concatenate([raw[i * 4 + k, 0] for i in range(8)], axis=0)
            if k:
                block = (block.astype(FULL) - mm(low[k - 1, :, 0 : k * n], upper[0 : k * n, :])).astype(HALF)
            upper[cut(k, n), :] = mm(w[k], block).astype(HALF)

        @pl.when(jnp.logical_not(present))
        def _():
            upper[cut(k, n), :] = jnp.zeros((n, n), HALF)

    @pl.when(shape[p, j] != 0)
    def _():
        out[...] = own[0].astype(FULL) - mm(left[...], upper[...])

    @pl.when(shape[p, j] == 0)
    def _():
        out[...] = own[0].astype(FULL)

    @pl.when(jnp.logical_and(p < STEPS, j > p))
    def _():
        out[...] = upper[pl.ds(pl.multiple_of(jnp.minimum(p, 3) * n, n), n), :].astype(FULL)

    @pl.when(jnp.logical_and(j < STEPS, p > j))
    def _():
        out[...] = left[:, pl.ds(pl.multiple_of(jnp.minimum(j, 3) * n, n), n)].astype(FULL)

    for i in range(4):

        @pl.when(c == i)
        def _():
            whole_out[:, i, :] = out[...]


def factor(ids, shape, corner, row, v, w):
    n = v.shape[1]
    vmem = pl.BlockSpec(memory_space=pltpu.VMEM)
    smem = pl.BlockSpec(memory_space=pltpu.SMEM)
    return pl.pallas_call(
        factor_kernel,
        out_shape=(
            jax.ShapeDtypeStruct((3, n, 3 * n), HALF),
            jax.ShapeDtypeStruct((n, 4 * n), HALF),
        ),
        in_specs=[smem, smem] + [vmem] * 12,
        out_specs=(vmem, vmem),
        scratch_shapes=[pltpu.VMEM((3 * n, 4 * n), HALF)],
        compiler_params=pltpu.CompilerParams(vmem_limit_bytes=VMEM_LIMIT),
        cost_estimate=pl.CostEstimate(flops=60 * n**3, bytes_accessed=18 * 2**20, transcendentals=0),
    )(ids, shape, *corner, *row, v, w)


def columns(ids, shape, raw, own, low, left, w):
    n = w.shape[1]
    smem = pl.BlockSpec(memory_space=pltpu.SMEM)
    whole = lambda a: pl.BlockSpec(a.shape, lambda c: (0,) * a.ndim, pipeline_mode=pl.Buffered(1))
    return pl.pallas_call(
        column_kernel,
        grid=(4,),
        out_shape=jax.ShapeDtypeStruct((n, 4, n), FULL),
        in_specs=[
            smem,
            smem,
            pl.BlockSpec((32, 1, n // 8, n), lambda c: (0, c, 0, 0)),
            pl.BlockSpec((1, n, n), lambda c: (c, 0, 0)),
            whole(low),
            whole(left),
            whole(w),
        ],
        out_specs=pl.BlockSpec((n, 4, n), lambda c: (0, 0, 0)),
        scratch_shapes=[pltpu.VMEM((4 * n, n), HALF), pltpu.VMEM((n, n), FULL)],
        compiler_params=pltpu.CompilerParams(vmem_limit_bytes=VMEM_LIMIT),
        cost_estimate=pl.CostEstimate(flops=112 * n**3, bytes_accessed=24 * 2**20, transcendentals=0),
    )(ids, shape, raw, own, low, left, w)


def on_device(matrix, upper_inverse, lower_inverse, structure):
    p = lax.axis_index("prow")
    q = lax.axis_index("pcol")
    z, core = p // 4, lax.rem(q, 2)
    n = matrix.shape[1]
    part = n // 8
    own = jnp.transpose(matrix[0], (1, 0, 2))
    ids = jnp.stack([p, q]).astype(jnp.int32)

    piece = own[:, :part]
    came = {}
    for s in (1, 4, 5, 3, 6, 2, 7):
        to = [(i, i + 4 * s) for i in range(4)]
        came[s] = lax.ppermute(own[:, s * part : (s + 1) * part], "prow", to)
    row, came[1] = lax.optimization_barrier((own[0], came[1]))
    row_above, row_below = shift(row, "y-"), shift(row, "y+")
    for s in came:
        piece = jnp.where(z == s, came[s], piece)

    raw = lax.all_gather(piece, "prow")

    first = lax.ppermute(piece[0, : part // 2], "pcol", [(i, 2 * i) for i in range(4)])
    second = lax.ppermute(piece[0, part // 2 :], "pcol", [(i, 2 * i + 1) for i in range(4)])
    corner = jnp.where(core == 0, first, second)
    corner = [corner, shift(corner, "x-"), shift(shift(corner, "x-"), "x-"), shift(corner, "x+")]
    gap = lax.rem(q // 2 - p % 4 + 4, 4)
    corner = jnp.stack([jnp.where(i < gap, corner[i], corner[i + 1]) for i in range(3)])
    corner, row_above, row_below = lax.optimization_barrier((corner, row_above, row_below))
    corner = jnp.stack(around_eight(corner))
    above, below = shift(corner, "y-"), shift(corner, "y+")
    row_far = [shift(row_below[: n // 2], "y+"), shift(row_above[n // 2 :], "y-")]
    row = jnp.stack([own[0], row_above, jnp.concatenate(row_far, axis=0), row_below])
    row = [row, shift(row, "c")]
    above, below, row = lax.optimization_barrier((above, below, row))
    far = jnp.concatenate([shift(below[:4], "y+"), shift(above[4:], "y-")], axis=0)
    corner = [corner, above, far, below]
    corner = corner + [shift(block, "c") for block in corner]

    low, left = factor(ids, structure, corner, row, upper_inverse, lower_inverse)
    out = columns(ids, structure, raw, own, low, left, lower_inverse)
    return out[None]


def solution(mesh):
    return jax.shard_map(
        on_device,
        mesh=mesh,
        in_specs=(P(None, "prow", None, "pcol"), P(), P(), P()),
        out_specs=P(None, "prow", None, "pcol"),
        check_vma=False,
    )
```

```python
import functools

import jax
import jax.numpy as jnp
from jax import lax
from jax.experimental import pallas as pl
from jax.experimental.pallas import tpu as pltpu
from jax.sharding import PartitionSpec as P

STEPS = 4
HALF = jnp.bfloat16
FULL = jnp.float32
VMEM_LIMIT = 56 * 1024 * 1024


def mm(a, b):
    return jnp.dot(a, b, preferred_element_type=FULL)


def shift(block, way):
    move = 1 if way[-1] == "+" else -1
    if way[0] == "z":
        return lax.ppermute(block, "prow", [(i, (i + 4 * move) % 32) for i in range(32)])
    if way[0] == "x":
        return lax.ppermute(block, "prow", [(i, i // 4 * 4 + (i + move) % 4) for i in range(32)])
    if way[0] == "y":
        return lax.ppermute(block, "pcol", [(i, (i + 2 * move) % 8) for i in range(8)])
    return lax.ppermute(block, "pcol", [(i, i ^ 1) for i in range(8)])


def around_eight(block):
    half = block.shape[1] // 2
    up, down = [block], [block]
    for _ in range(3):
        up.append(shift(up[-1], "z+"))
        down.append(shift(down[-1], "z-"))
    far = [shift(up[3][:, :half], "z+"), shift(down[3][:, half:], "z-")]
    return up + [jnp.concatenate(far, axis=1)] + down[:0:-1]


def cut(k, n):
    return slice(k * n, (k + 1) * n)


def factor_kernel(ids, shape, *refs):
    mine, other, (row_mine, row_other, v, w, low, left, up) = refs[:4], refs[4:8], refs[8:]
    n = v.shape[1]
    p, q = ids[0], ids[1]
    z, x, y, core = p // 4, lax.rem(p, 4), q // 2, lax.rem(q, 2)

    def raw_corner(k, m):
        dx, dy, gap = lax.rem(k - x + 4, 4), lax.rem(m - y + 4, 4), lax.rem(m - x + 4, 4)
        at = jnp.where(dx < gap, dx, jnp.maximum(dx - 1, 0))
        odd, upper_half = lax.rem(dy, 2) == 1, dy >= 2

        def pick(four, away):
            low_pair = jnp.where(odd, four[1][away, at], four[0][away, at])
            return jnp.where(upper_half, jnp.where(odd, four[3][away, at], four[2][away, at]), low_pair)

        parts = []
        for i in range(8):
            away = lax.rem(z - i + 8, 8)
            here, there = pick(mine, away), pick(other, away)
            parts += [jnp.where(core == 0, here, there), jnp.where(core == 0, there, here)]
        return jnp.concatenate(parts, axis=0)

    def raw_row(k):
        dy = lax.rem(k // 2 - y + 4, 4)
        return jnp.where(core == k % 2, row_mine[dy], row_other[dy])

    def fill(ref, rows, cols, present, make):
        @pl.when(present)
        def _():
            ref[rows, cols] = make().astype(HALF)

        @pl.when(jnp.logical_not(present))
        def _():
            ref[rows, cols] = jnp.zeros((n, n), HALF)

    def less(block, a, b):
        return (block.astype(FULL) - mm(a, b)).astype(HALF)

    for k in range(3):
        for i in range(k + 1, 4):

            def make_low():
                block = raw_corner(i, k)
                if k:
                    block = less(block, low[i - 1, :, 0 : k * n], up[0 : k * n, cut(k, n)])
                return mm(block, v[k])

            def make_up():
                block = raw_corner(k, i)
                if k:
                    block = less(block, low[k - 1, :, 0 : k * n], up[0 : k * n, cut(i, n)])
                return mm(w[k], block)

            fill(low.at[i - 1], slice(None), cut(k, n), shape[i, k] != 0, make_low)
            fill(up, cut(k, n), cut(i, n), shape[k, i] != 0, make_up)
    for k in range(4):

        def make_left():
            block = raw_row(k)
            if k:
                block = less(block, left[:, 0 : k * n], up[0 : k * n, cut(k, n)])
            return mm(block, v[k])

        fill(left, slice(None), cut(k, n), jnp.logical_and(p > k, shape[p, k] != 0), make_left)


def column_kernel(ids, shape, raw, own, low, left, w, whole_out, upper, out):
    n = w.shape[1]
    p, q = ids[0], ids[1]
    c = pl.program_id(0)
    j = c * 8 + q
    for k in range(4):
        present = jnp.logical_and(j > k, shape[k, j] != 0)

        @pl.when(present)
        def _():
            block = jnp.concatenate([raw[i * 4 + k, 0] for i in range(8)], axis=0)
            if k:
                block = (block.astype(FULL) - mm(low[k - 1, :, 0 : k * n], upper[0 : k * n, :])).astype(HALF)
            upper[cut(k, n), :] = mm(w[k], block).astype(HALF)

        @pl.when(jnp.logical_not(present))
        def _():
            upper[cut(k, n), :] = jnp.zeros((n, n), HALF)

    @pl.when(shape[p, j] != 0)
    def _():
        out[...] = own[0].astype(FULL) - mm(left[...], upper[...])

    @pl.when(shape[p, j] == 0)
    def _():
        out[...] = own[0].astype(FULL)

    @pl.when(jnp.logical_and(p < STEPS, j > p))
    def _():
        out[...] = upper[pl.ds(pl.multiple_of(jnp.minimum(p, 3) * n, n), n), :].astype(FULL)

    @pl.when(jnp.logical_and(j < STEPS, p > j))
    def _():
        out[...] = left[:, pl.ds(pl.multiple_of(jnp.minimum(j, 3) * n, n), n)].astype(FULL)

    for i in range(4):

        @pl.when(c == i)
        def _():
            whole_out[:, i, :] = out[...]


def factor(ids, shape, corner, row, v, w):
    n = v.shape[1]
    vmem = pl.BlockSpec(memory_space=pltpu.VMEM)
    smem = pl.BlockSpec(memory_space=pltpu.SMEM)
    return pl.pallas_call(
        factor_kernel,
        out_shape=(
            jax.ShapeDtypeStruct((3, n, 3 * n), HALF),
            jax.ShapeDtypeStruct((n, 4 * n), HALF),
        ),
        in_specs=[smem, smem] + [vmem] * 12,
        out_specs=(vmem, vmem),
        scratch_shapes=[pltpu.VMEM((3 * n, 4 * n), HALF)],
        compiler_params=pltpu.CompilerParams(vmem_limit_bytes=20 * 1024 * 1024),
        cost_estimate=pl.CostEstimate(flops=60 * n**3, bytes_accessed=18 * 2**20, transcendentals=0),
    )(ids, shape, *corner, *row, v, w)


def columns(ids, shape, raw, own, low, left, w):
    n = w.shape[1]
    smem = pl.BlockSpec(memory_space=pltpu.SMEM)
    whole = lambda a: pl.BlockSpec(a.shape, lambda c: (0,) * a.ndim, pipeline_mode=pl.Buffered(1))
    return pl.pallas_call(
        column_kernel,
        grid=(4,),
        out_shape=jax.ShapeDtypeStruct((n, 4, n), FULL),
        in_specs=[
            smem,
            smem,
            pl.BlockSpec((32, 1, n // 8, n), lambda c: (0, c, 0, 0)),
            pl.BlockSpec((1, n, n), lambda c: (c, 0, 0)),
            whole(low),
            whole(left),
            whole(w),
        ],
        out_specs=pl.BlockSpec((n, 4, n), lambda c: (0, 0, 0)),
        scratch_shapes=[pltpu.VMEM((4 * n, n), HALF), pltpu.VMEM((n, n), FULL)],
        compiler_params=pltpu.CompilerParams(vmem_limit_bytes=VMEM_LIMIT),
        cost_estimate=pl.CostEstimate(flops=112 * n**3, bytes_accessed=24 * 2**20, transcendentals=0),
    )(ids, shape, raw, own, low, left, w)


def on_device(matrix, upper_inverse, lower_inverse, structure):
    p = lax.axis_index("prow")
    q = lax.axis_index("pcol")
    z, core = p // 4, lax.rem(q, 2)
    n = matrix.shape[1]
    part = n // 8
    own = jnp.transpose(matrix[0], (1, 0, 2))
    ids = jnp.stack([p, q]).astype(jnp.int32)

    piece = matrix[0, :part]
    came = {}
    for s in (1, 4, 5, 3, 6, 2, 7):
        to = [(i, i + 4 * s) for i in range(4)]
        came[s] = lax.ppermute(matrix[0, s * part : (s + 1) * part], "prow", to)
    row, came[1] = lax.optimization_barrier((own[0], came[1]))
    row_above, row_below = shift(row, "y-"), shift(row, "y+")
    for s in came:
        piece = jnp.where(z == s, came[s], piece)
    piece = jnp.transpose(piece, (1, 0, 2))

    raw = lax.all_gather(piece, "prow")

    first = lax.ppermute(piece[0, : part // 2], "pcol", [(i, 2 * i) for i in range(4)])
    second = lax.ppermute(piece[0, part // 2 :], "pcol", [(i, 2 * i + 1) for i in range(4)])
    corner = jnp.where(core == 0, first, second)
    corner = [corner, shift(corner, "x-"), shift(shift(corner, "x-"), "x-"), shift(corner, "x+")]
    gap = lax.rem(q // 2 - p % 4 + 4, 4)
    corner = jnp.stack([jnp.where(i < gap, corner[i], corner[i + 1]) for i in range(3)])
    corner, row_above, row_below = lax.optimization_barrier((corner, row_above, row_below))
    corner = jnp.stack(around_eight(corner))
    above, below = shift(corner, "y-"), shift(corner, "y+")
    row_far = [shift(row_below[: n // 2], "y+"), shift(row_above[n // 2 :], "y-")]
    row = jnp.stack([own[0], row_above, jnp.concatenate(row_far, axis=0), row_below])
    row = [row, shift(row, "c")]
    above, below, row = lax.optimization_barrier((above, below, row))
    far = jnp.concatenate([shift(below[:4], "y+"), shift(above[4:], "y-")], axis=0)
    corner = [corner, above, far, below]
    corner = corner + [shift(block, "c") for block in corner]

    low, left = factor(ids, structure, corner, row, upper_inverse, lower_inverse)
    out = columns(ids, structure, raw, own, low, left, lower_inverse)
    return out[None]


def solution(mesh):
    return jax.shard_map(
        on_device,
        mesh=mesh,
        in_specs=(P(None, "prow", None, "pcol"), P(), P(), P()),
        out_specs=P(None, "prow", None, "pcol"),
        check_vma=False,
    )
```
